32 devices in a mesh: ctx: 8 (over y, x, core), head: 4 (over z).
Axes of the slice: x: 2, y: 2, z: 4, core: 2. Of those that a mesh axis runs over, the one named last changes fastest.
Arguments:
- queries: bfloat16 [2048, 2560], P('ctx', 'head'), may hold values from -6 to 6
- keys: bfloat16 [2048, 2560], P('ctx', 'head'), may hold values from -6 to 6
- values: bfloat16 [2048, 2560], P('ctx', 'head'), may hold values from -16 to 16
- out_weight: bfloat16 [2560, 2560], P('head'), may hold values from -0.125 to 0.125
- cotangent: bfloat16 [2048, 2560], P('ctx', 'head'), may hold values from -16 to 16
- contacts: int32 [16, 16], replicated, may hold values 0 or 1
- chains: int32 [16], replicated, may hold values from 0 to 3, never falling along the last dimension, each value on 1 to 8 neighbouring positions
Outputs:
- mixed: bfloat16 [2048, 2560], P('ctx', 'head')
- query_grad: bfloat16 [2048, 2560], P('ctx', 'head')
- key_grad: bfloat16 [2048, 2560], P('ctx', 'head')
- value_grad: bfloat16 [2048, 2560], P('ctx', 'head')
The draws below stay inside these ranges and needn't reach their ends.
Inputs may be any that keep to these rules, and one draw needn't show every extreme that they name: `chains`: chain numbers never fall along the blocks; each chain has 1 to 8 blocks, one exactly 8.
All inputs are finite; a program needn't handle non-finite values.
Results may differ from the reference program's by a relative error of at most 0.02.
Values may be sent and summed in bfloat16 or wider, within the bound.
A program may use at most 192 MiB of HBM per device.

```python
import math
import jax
import jax.numpy as jnp
import numpy as np
from jax import lax

HEAD_SIZE = 128
HEADS = 20
D_MODEL = 2560
BLOCK = 128
CHAINS = 4
ROWS_DEV = 256
LENGTH = 2048
NBLOCKS = 16
N_CTX = 8


def drawn_pair(key):
    first = jax.random.fold_in(key, 11)
    second = jax.random.fold_in(key, 12)
    query_part = jnp.clip(jax.random.normal(first, (LENGTH, D_MODEL), jnp.float32), -5.0, 5.0)
    key_part = jnp.clip(jax.random.normal(second, (LENGTH, D_MODEL), jnp.float32), -5.0, 5.0)
    return (query_part, key_part)


def draw_queries(key, part):
    return drawn_pair(key)[0].astype(jnp.bfloat16)


def draw_keys(key, part):
    return drawn_pair(key)[1].astype(jnp.bfloat16)


def plant(drawn, own_key, least, largest):
    shape = drawn.shape
    index_at = [jax.random.randint(jax.random.fold_in(own_key, axis), (), 0, shape[axis]) for axis in range(len(shape))]
    drawn = drawn.at[tuple(index_at)].set(least)
    longest = shape.index(max(shape))
    index_at[longest] = (index_at[longest] + 1) % shape[longest]
    return drawn.at[tuple(index_at)].set(largest)


def steps_of(key, dims, shards, least, largest):
    loudness, own = 1.0, jax.random.fold_in(key, 6)
    for dim, shards_of in shards:
        heights = jnp.exp(jax.random.uniform(jax.random.fold_in(own, dim), (shards_of,), jnp.float32, least / len(shards), largest / len(shards)))
        loudness = loudness * jnp.repeat(heights, dims[dim] // shards_of).reshape([-1 if axis == dim else 1 for axis in range(len(dims))])
    return loudness


def length_profile(amount, total, limit, slope):
    portions = [(1 << 20) // math.isqrt(rank ** slope) + 1 for rank in range(2, amount + 1)]
    rest, holding = total - limit - (amount - 1), [1] * (amount - 1)
    while rest > 0:
        candidates = [i for i in range(amount - 1) if holding[i] < limit]
        whole, remaining = sum([portions[i] for i in candidates]), rest
        for i in candidates:
            extra = min(limit - holding[i], max(1, remaining * portions[i] // whole), rest)
            holding[i] = holding[i] + extra
            rest = rest - extra
    return np.array([limit] + holding)


def uneven_parts(own_key, amount, total, limit, lean):
    if amount == 2:
        one = jax.random.randint(own_key, (), max(1, total - limit), min(limit, total - 1) + 1)
        return jnp.stack([one, total - one])
    lengths = jnp.asarray(length_profile(amount, total, limit, lean), jnp.int32)
    pairs = (amount - 1) // 2
    donor, receiver = lengths[1:1 + 2 * pairs:2], lengths[2:2 + 2 * pairs:2]
    margin = jnp.minimum(donor - 1, limit - receiver)
    passed = jax.random.randint(jax.random.fold_in(own_key, 1), (pairs,), 0, 1 << 20) % (margin + 1)
    lengths = lengths.at[1:1 + 2 * pairs:2].set(donor - passed).at[2:2 + 2 * pairs:2].set(receiver + passed)
    return lengths[jax.random.permutation(jax.random.fold_in(own_key, 2), amount)]


def normal_values(rng, extent, deviation, limit, pieces=(), dtype=jnp.bfloat16):
    gain = steps_of(rng, extent, pieces, -0.22, 0.18) if pieces else 1.0
    values = jax.random.normal(rng, extent, jnp.float32) * deviation * gain
    return jnp.minimum(jnp.maximum(values, -limit), limit).astype(dtype)


def setup_inputs(seed: int = 0) -> dict:
    arg_keys = jax.random.split(jax.random.key(seed), 8)
    return {
        "queries": draw_queries(jax.random.fold_in(arg_keys[7], 71), 0),
        "keys": draw_keys(jax.random.fold_in(arg_keys[7], 71), 0),
        "values": normal_values(arg_keys[2], (LENGTH, D_MODEL), 4.0, 16.0, ((0, 8), (1, 4))),
        "out_weight": normal_values(arg_keys[3], (D_MODEL, D_MODEL), D_MODEL ** -0.5, 0.125, ((0, 4),)),
        "cotangent": normal_values(arg_keys[4], (LENGTH, D_MODEL), 4.0, 16.0, ((0, 8), (1, 4))),
        "contacts": plant((jax.random.randint(arg_keys[5], (NBLOCKS, NBLOCKS), 0, 8) < 1).astype(jnp.int32), jax.random.fold_in(arg_keys[5], 1), 0, 1),
        "chains": jnp.searchsorted(jnp.cumsum(uneven_parts(arg_keys[6], CHAINS, NBLOCKS, NBLOCKS // 2, 2)), jnp.arange(NBLOCKS), side="right").astype(jnp.int32),
    }


NEG = -1e30


def rounded(value):
    return lax.optimization_barrier(value.astype(jnp.bfloat16)).astype(jnp.float32)


def reference(queries, keys, values, out_weight, cotangent, contacts, chains):
    scale = HEAD_SIZE ** -0.5
    allowed = jnp.logical_or(chains[:, None] == chains[None, :], contacts > 0)
    keep = jnp.repeat(jnp.repeat(allowed, BLOCK, axis=0), BLOCK, axis=1)

    def split(field):
        return field.reshape(LENGTH, HEADS, HEAD_SIZE).transpose(1, 0, 2)

    def join(field):
        return field.transpose(1, 0, 2).reshape(LENGTH, D_MODEL)

    q_heads, k_heads, v_heads = split(queries), split(keys), split(values)

    def scores_of(q_one, k_one):
        product = jnp.dot(q_one, k_one.T, preferred_element_type=jnp.float32) * scale
        return jnp.where(keep, product, NEG)

    def forward_head(operands):
        q_one, k_one, v_one = operands
        scores = scores_of(q_one, k_one)
        best = jnp.max(scores, axis=1)
        weights = jnp.where(keep, jnp.exp(scores - best[:, None]), 0.0)
        total = jnp.sum(weights, axis=1)
        mixed_one = jnp.dot(weights.astype(jnp.bfloat16), v_one, preferred_element_type=jnp.float32) / total[:, None]
        return mixed_one.astype(jnp.bfloat16), best + jnp.log(total)

    attended, lse = lax.map(forward_head, (q_heads, k_heads, v_heads))
    mixed = jnp.dot(join(attended), out_weight, preferred_element_type=jnp.float32).astype(jnp.bfloat16)
    grads = lax.dot_general(cotangent, out_weight, (((1,), (1,)), ((), ())), preferred_element_type=jnp.float32).astype(jnp.bfloat16)
    g_heads = split(grads)

    def backward_head(operands):
        q_one, k_one, v_one, g_one, o_one, l_one = operands
        scores = scores_of(q_one, k_one)
        probs = jnp.where(keep, jnp.exp(scores - l_one[:, None]), 0.0)
        delta = jnp.sum(g_one.astype(jnp.float32) * o_one.astype(jnp.float32), axis=1)
        dprob = jnp.dot(g_one, v_one.T, preferred_element_type=jnp.float32)
        dscore = (probs * (dprob - delta[:, None])).astype(jnp.bfloat16)
        dscore_wide = lax.optimization_barrier(dscore).astype(jnp.float32)
        probs_wide = lax.optimization_barrier(probs.astype(jnp.bfloat16)).astype(jnp.float32)
        groups = N_CTX
        q_wide = q_one.astype(jnp.float32).reshape(groups, ROWS_DEV, HEAD_SIZE)
        k_wide = k_one.astype(jnp.float32).reshape(groups, ROWS_DEV, HEAD_SIZE)
        g_wide = g_one.astype(jnp.float32).reshape(groups, ROWS_DEV, HEAD_SIZE)
        q_terms = jnp.einsum("lgr,grd->gld", dscore_wide.reshape(LENGTH, groups, ROWS_DEV), k_wide) * scale
        k_terms = jnp.einsum("grk,grd->gkd", dscore_wide.reshape(groups, ROWS_DEV, LENGTH), q_wide) * scale
        v_terms = jnp.einsum("grk,grd->gkd", probs_wide.reshape(groups, ROWS_DEV, LENGTH), g_wide)
        q_grad = jnp.sum(rounded(q_terms), axis=0).astype(jnp.bfloat16)
        k_grad = jnp.sum(rounded(k_terms), axis=0).astype(jnp.bfloat16)
        v_grad = jnp.sum(rounded(v_terms), axis=0).astype(jnp.bfloat16)
        return q_grad, k_grad, v_grad

    q_grads, k_grads, v_grads = lax.map(backward_head, (q_heads, k_heads, v_heads, g_heads, attended, lse))
    return (mixed, join(q_grads), join(k_grads), join(v_grads))
```

```python
import functools
import math

import jax
import jax.numpy as jnp
from jax import lax
from jax.experimental import pallas as pl
from jax.experimental.pallas import tpu as pltpu
from jax.sharding import PartitionSpec as P

SIZE = 128
BLOCK = 128
NEG = -1e30
SCALE = SIZE ** (-0.5)
SCALE2 = SCALE * math.log2(math.e)
MESH = pl.DeviceIdType.MESH

NT = (((1,), (1,)), ((), ()))
TN = (((0,), (0,)), ((), ()))
NN = (((1,), (0,)), ((), ()))


def mm(a, b, dims):
    return lax.dot_general(a, b, dims, preferred_element_type=jnp.float32)


def kernel(
    chips, nhead, heads, unroll,
    bias, q, k, v, w, cot,
    mixed, qg, kg, vg,
    kv, probs, sbuf, att, att_t, inv, g_t, sib, rem, wbuf, cbuf, mstage, mrecv,
    lsem, wsem, clocal, gsend, grecv, csend, crecv, msend, mrsem, ssend, srecv, rsend, rrecv,
):
    rows = q.shape[0]
    width = heads * SIZE
    n = chips * 2
    bpr = rows // BLOCK
    me = lax.axis_index("ctx")
    mh = lax.axis_index("head")
    core = lax.rem(me, 2)
    chip = lax.div(me, 2)
    other = 1 - core
    sibling = chip * 2 + other
    mine = core * chips + chip

    def chip_at(d):
        return lax.rem(chip + d, chips)

    def head_at(d):
        return lax.rem(mh + d, nhead)

    def cols(h):
        return pl.ds(pl.multiple_of(h * SIZE, SIZE), SIZE)

    def remote(src, dst, ssem, rsem, where):
        return pltpu.make_async_remote_copy(
            src_ref=src, dst_ref=dst, send_sem=ssem, recv_sem=rsem,
            device_id=where, device_id_type=MESH,
        )

    def own_k(h):
        return pltpu.make_async_copy(k.at[:, cols(h)], kv.at[h, mine, 0], lsem.at[0, h])

    def own_v(h):
        return pltpu.make_async_copy(v.at[:, cols(h)], kv.at[h, mine, 1], lsem.at[1, h])

    def own_cot():
        return pltpu.make_async_copy(cot, cbuf.at[mh], clocal)

    def load_w(c):
        return pltpu.make_async_copy(
            w.at[:, pl.ds(c * width, width)], wbuf.at[c], wsem.at[c]
        )

    def direct(h, d):
        return remote(
            kv.at[h, mine], kv.at[h, mine], gsend.at[h, d - 1], grecv.at[h, mine],
            {"ctx": chip_at(d) * 2 + core},
        )

    def forward(h, d):
        slot = core * chips + chip_at(d)
        return remote(
            kv.at[h, slot], kv.at[h, slot], gsend.at[h, chips - 1 + d], grecv.at[h, slot],
            {"ctx": sibling},
        )

    def arrived(h, slot):
        return remote(
            kv.at[h, slot], kv.at[h, slot], gsend.at[h, 0], grecv.at[h, slot], {"ctx": sibling}
        )

    def cot_copy(d):
        return remote(
            cbuf.at[mh], cbuf.at[mh], csend.at[d - 1], crecv.at[mh], {"head": head_at(d)}
        )

    def cot_arrived(d):
        src = head_at(d)
        return remote(
            cbuf.at[src], cbuf.at[src], csend.at[d - 1], crecv.at[src], {"head": src}
        )

    def mixed_copy(d):
        return remote(
            mstage.at[d - 1], mrecv.at[d - 1], msend.at[d - 1], mrsem.at[d - 1],
            {"head": head_at(d)},
        )

    def sib_copy(h):
        return remote(
            kv.at[h, pl.ds(other * chips, chips)], sib.at[h], ssend.at[h], srecv.at[h],
            {"ctx": sibling},
        )

    def rem_copy(h, d):
        return remote(
            kv.at[h, core * chips + chip_at(d)], rem.at[h, d - 1],
            rsend.at[h, d - 1], rrecv.at[h, d - 1],
            {"ctx": chip_at(d) * 2 + core},
        )

    own_cot().start()

    @pl.loop(0, heads)
    def _(h):
        own_k(h).start()
        own_v(h).start()

    for c in range(nhead):
        load_w(c).start()

    barrier = pltpu.get_barrier_semaphore()
    for d in range(1, nhead):
        pl.semaphore_signal(barrier, inc=1, device_id={"head": head_at(d)}, device_id_type=MESH)
    for d in range(1, chips):
        pl.semaphore_signal(
            barrier, inc=1, device_id={"ctx": chip_at(d) * 2 + core}, device_id_type=MESH
        )
    pl.semaphore_signal(barrier, inc=1, device_id={"ctx": sibling}, device_id_type=MESH)
    pl.semaphore_wait(barrier, nhead - 1 + chips)

    own_cot().wait()
    for d in range(1, nhead):
        cot_copy(d).start()

    @pl.loop(0, heads)
    def _(h):
        own_k(h).wait()
        own_v(h).wait()
        for d in range(1, chips):
            direct(h, d).start()
        forward(h, 0).start()

    @pl.loop(0, heads)
    def _(h):
        for d in range(1, chips):
            arrived(h, core * chips + chip_at(d)).wait_recv()
            forward(h, d).start()
        for c in range(chips):
            arrived(h, other * chips + c).wait_recv()
        qh = q[:, cols(h)]

        def scores(i, best):
            s = mm(kv[h, i, 0], qh, NT)
            s = s.reshape(bpr, BLOCK, rows) + bias[i][:, None, :]
            s = s.reshape(rows, rows)
            sbuf[i] = s
            return jnp.maximum(best, jnp.max(s.reshape(rows // 8, 8, rows), axis=0))

        best = lax.fori_loop(
            0, n, scores, jnp.full((8, rows), 2 * NEG, jnp.float32), unroll=unroll
        )
        best = jnp.max(best, axis=0, keepdims=True)

        def weigh(i, carry):
            total, acc = carry
            p = jnp.exp2((sbuf[i] - best) * SCALE2)
            total = total + jnp.sum(p.reshape(rows // 8, 8, rows), axis=0)
            pb = p.astype(jnp.bfloat16)
            probs[h, i] = pb
            return total, acc + mm(kv[h, i, 1], pb, TN)

        total, acc = lax.fori_loop(
            0, n, weigh,
            (jnp.zeros((8, rows), jnp.float32), jnp.zeros((SIZE, rows), jnp.float32)),
            unroll=unroll,
        )
        scale = 1.0 / jnp.sum(total, axis=0, keepdims=True)
        inv[h] = scale
        out = acc * scale
        att_t[h] = out
        att[:, cols(h)] = out.T.astype(jnp.bfloat16)

    for c in range(nhead):
        load_w(c).wait()
    attended = att[...]
    for d in range(1, nhead):
        mstage[d - 1] = mm(attended, wbuf[head_at(d)], NN).astype(jnp.bfloat16)
        mixed_copy(d).start()

    g_t[...] = mm(wbuf[mh], cbuf[mh], NT)
    for d in range(1, nhead):
        cot_arrived(d).wait_recv()
        g_t[...] += mm(wbuf[head_at(d)], cbuf[head_at(d)], NT)

    def combine(h):
        sib_copy(h).wait_recv()
        for d in range(1, chips + 1):
            c = chip_at(d)
            slot = core * chips + c
            kv[h, slot] = (
                kv[h, slot].astype(jnp.float32) + sib[h, c].astype(jnp.float32)
            ).astype(jnp.bfloat16)
            if d < chips:
                rem_copy(h, d).start()

    @pl.loop(0, heads)
    def _(h):
        for d in range(1, chips):
            direct(h, d).wait_send()
        for d in range(chips):
            forward(h, d).wait_send()
        qh = q[:, cols(h)]
        at = att_t[h].astype(jnp.bfloat16).astype(jnp.float32)
        gt = g_t[pl.ds(pl.multiple_of(h * SIZE, SIZE), SIZE), :].astype(jnp.bfloat16)
        gt = gt.astype(jnp.float32) * inv[h]
        delta = jnp.sum(gt * at, axis=0, keepdims=True)
        gn = gt.T.astype(jnp.bfloat16)
        gt = gt.astype(jnp.bfloat16)

        def step(i, acc):
            kb, vb, pb = kv[h, i, 0], kv[h, i, 1], probs[h, i]
            dp = mm(vb, gt, NN)
            ds = (pb.astype(jnp.float32) * (dp - delta)).astype(jnp.bfloat16)
            kv[h, i, 0] = (mm(ds, qh, NN) * SCALE).astype(jnp.bfloat16)
            kv[h, i, 1] = mm(pb, gn, NN).astype(jnp.bfloat16)
            return acc + mm(kb, ds, TN)

        acc = lax.fori_loop(
            0, n, step, jnp.zeros((SIZE, rows), jnp.float32), unroll=unroll
        )
        qg[:, cols(h)] = (acc.T * SCALE).astype(jnp.bfloat16)
        sib_copy(h).start()

        @pl.when(h > 0)
        def _():
            combine(h - 1)

    combine(heads - 1)

    total = mm(attended, wbuf[mh], NN)
    for d in range(1, nhead):
        mixed_copy(d).wait_recv()
        total += mrecv[d - 1].astype(jnp.float32)
    mixed[...] = total.astype(jnp.bfloat16)

    @pl.loop(0, heads)
    def _(h):
        total = kv[h, mine].astype(jnp.float32)
        for d in range(1, chips):
            rem_copy(h, d).wait_recv()
            total += rem[h, d - 1].astype(jnp.float32)
        kg[:, cols(h)] = total[0].astype(jnp.bfloat16)
        vg[:, cols(h)] = total[1].astype(jnp.bfloat16)

    for d in range(1, nhead):
        cot_copy(d).wait_send()
        mixed_copy(d).wait_send()

    @pl.loop(0, heads)
    def _(h):
        sib_copy(h).wait_send()
        for d in range(1, chips):
            rem_copy(h, d).wait_send()


def per_device(queries, keys, values, out_weight, cotangent, contacts, chains):
    rows, width = queries.shape
    heads = width // SIZE
    n = lax.axis_size("ctx")
    nhead = lax.axis_size("head")
    chips = n // 2
    bpr = rows // BLOCK
    allowed = jnp.logical_or(chains[:, None] == chains[None, :], contacts > 0)
    own = lax.dynamic_slice(
        allowed, (lax.axis_index("ctx") * bpr, 0), (bpr, allowed.shape[1])
    )
    bias = jnp.where(own, 0.0, NEG).astype(jnp.float32)
    bias = bias.reshape(bpr, chips, 2, bpr).transpose(2, 1, 3, 0)
    bias = jnp.repeat(bias.reshape(n, bpr, bpr), BLOCK, axis=2)
    out = jax.ShapeDtypeStruct((rows, width), jnp.bfloat16)
    vmem = pl.BlockSpec(memory_space=pltpu.VMEM)
    hbm = pl.BlockSpec(memory_space=pl.ANY)
    bf16, f32 = jnp.bfloat16, jnp.float32
    dma = pltpu.SemaphoreType.DMA
    flops = 2 * rows * n * rows * width * 6 + 4 * rows * width * width * nhead
    return pl.pallas_call(
        functools.partial(kernel, chips, nhead, heads, 4),
        out_shape=(out, out, out, out),
        in_specs=[vmem, vmem, hbm, hbm, hbm, hbm],
        out_specs=(vmem, vmem, vmem, vmem),
        scratch_shapes=[
            pltpu.VMEM((heads, n, 2, rows, SIZE), bf16),
            pltpu.VMEM((heads, n, rows, rows), bf16),
            pltpu.VMEM((n, rows, rows), f32),
            pltpu.VMEM((rows, width), bf16),
            pltpu.VMEM((heads, SIZE, rows), f32),
            pltpu.VMEM((heads, 1, rows), f32),
            pltpu.VMEM((width, rows), f32),
            pltpu.VMEM((heads, chips, 2, rows, SIZE), bf16),
            pltpu.VMEM((heads, chips - 1, 2, rows, SIZE), bf16),
            pltpu.VMEM((nhead, width, width), bf16),
            pltpu.VMEM((nhead, rows, width), bf16),
            pltpu.VMEM((nhead - 1, rows, width), bf16),
            pltpu.VMEM((nhead - 1, rows, width), bf16),
            dma((2, heads)),
            dma((nhead,)),
            dma,
            dma((heads, 2 * chips - 1)),
            dma((heads, n)),
            dma((nhead - 1,)),
            dma((nhead,)),
            dma((nhead - 1,)),
            dma((nhead - 1,)),
            dma((heads,)),
            dma((heads,)),
            dma((heads, chips - 1)),
            dma((heads, chips - 1)),
        ],
        compiler_params=pltpu.CompilerParams(
            collective_id=0, has_side_effects=True, vmem_limit_bytes=60 * 2**20
        ),
        cost_estimate=pl.CostEstimate(
            flops=flops, bytes_accessed=16 * rows * width, transcendentals=rows * n * rows * heads
        ),
        name="attention",
    )(bias, queries, keys, values, out_weight, cotangent)


def solution(mesh):
    split = P("ctx", "head")
    return jax.shard_map(
        per_device,
        mesh=mesh,
        in_specs=(split, split, split, P("head", None), split, P(), P()),
        out_specs=(split, split, split, split),
        check_vma=False,
    )
```

```python
import functools
import math

import jax
import jax.numpy as jnp
from jax import lax
from jax.experimental import pallas as pl
from jax.experimental.pallas import tpu as pltpu
from jax.sharding import PartitionSpec as P

SIZE = 128
BLOCK = 128
NEG = -1e30
SCALE = SIZE ** (-0.5)
SCALE2 = SCALE * math.log2(math.e)
MESH = pl.DeviceIdType.MESH

NT = (((1,), (1,)), ((), ()))
TN = (((0,), (0,)), ((), ()))
NN = (((1,), (0,)), ((), ()))


def mm(a, b, dims):
    return lax.dot_general(a, b, dims, preferred_element_type=jnp.float32)


def kernel(
    chips, nhead, heads, unroll,
    chains, contacts, q, k, v, w, cot,
    mixed, qg, kg, vg,
    bias, kv, probs, sbuf, att, att_t, inv, g_t, sib, rem, wbuf, cbuf, mstage, mrecv,
    lsem, wsem, clocal, gsend, grecv, csend, crecv, msend, mrsem, ssend, srecv, rsend, rrecv,
):
    rows = q.shape[0]
    width = heads * SIZE
    n = chips * 2
    bpr = rows // BLOCK
    me = lax.axis_index("ctx")
    mh = lax.axis_index("head")
    core = lax.rem(me, 2)
    chip = lax.div(me, 2)
    other = 1 - core
    sibling = chip * 2 + other
    mine = core * chips + chip

    def chip_at(d):
        return lax.rem(chip + d, chips)

    def head_at(d):
        return lax.rem(mh + d, nhead)

    def cols(h):
        return pl.ds(pl.multiple_of(h * SIZE, SIZE), SIZE)

    def remote(src, dst, ssem, rsem, where):
        return pltpu.make_async_remote_copy(
            src_ref=src, dst_ref=dst, send_sem=ssem, recv_sem=rsem,
            device_id=where, device_id_type=MESH,
        )

    def own_k(h):
        return pltpu.make_async_copy(k.at[:, cols(h)], kv.at[h, mine, 0], lsem.at[0, h])

    def own_v(h):
        return pltpu.make_async_copy(v.at[:, cols(h)], kv.at[h, mine, 1], lsem.at[1, h])

    def own_cot():
        return pltpu.make_async_copy(cot, cbuf.at[mh], clocal)

    def load_w(c):
        return pltpu.make_async_copy(
            w.at[:, pl.ds(c * width, width)], wbuf.at[c], wsem.at[c]
        )

    def direct(h, d):
        return remote(
            kv.at[h, mine], kv.at[h, mine], gsend.at[h, d - 1], grecv.at[h, mine],
            {"ctx": chip_at(d) * 2 + core},
        )

    def forward(h, d):
        slot = core * chips + chip_at(d)
        return remote(
            kv.at[h, slot], kv.at[h, slot], gsend.at[h, chips - 1 + d], grecv.at[h, slot],
            {"ctx": sibling},
        )

    def arrived(h, slot):
        return remote(
            kv.at[h, slot], kv.at[h, slot], gsend.at[h, 0], grecv.at[h, slot], {"ctx": sibling}
        )

    def cot_copy(d):
        return remote(
            cbuf.at[mh], cbuf.at[mh], csend.at[d - 1], crecv.at[mh], {"head": head_at(d)}
        )

    def cot_arrived(d):
        src = head_at(d)
        return remote(
            cbuf.at[src], cbuf.at[src], csend.at[d - 1], crecv.at[src], {"head": src}
        )

    def mixed_copy(d):
        return remote(
            mstage.at[d - 1], mrecv.at[d - 1], msend.at[d - 1], mrsem.at[d - 1],
            {"head": head_at(d)},
        )

    def sib_copy(h):
        return remote(
            kv.at[h, pl.ds(other * chips, chips)], sib.at[h], ssend.at[h], srecv.at[h],
            {"ctx": sibling},
        )

    def rem_copy(h, d):
        return remote(
            kv.at[h, core * chips + chip_at(d)], rem.at[h, d - 1],
            rsend.at[h, d - 1], rrecv.at[h, d - 1],
            {"ctx": chip_at(d) * 2 + core},
        )

    own_cot().start()

    @pl.loop(0, heads)
    def _(h):
        own_k(h).start()
        own_v(h).start()

    for c in range(nhead):
        load_w(c).start()

    for core_of in range(2):
        for c in range(chips):
            for b in range(bpr):
                key_block = (c * 2 + core_of) * bpr + b
                for a in range(bpr):
                    query_block = me * bpr + a
                    keep = (chains[query_block] == chains[key_block]) | (
                        contacts[query_block, key_block] > 0
                    )
                    bias[core_of * chips + c, pl.ds(b, 1), pl.ds(a * BLOCK, BLOCK)] = jnp.full(
                        (1, BLOCK), jnp.where(keep, 0.0, NEG), jnp.float32
                    )

    barrier = pltpu.get_barrier_semaphore()
    for d in range(1, nhead):
        pl.semaphore_signal(barrier, inc=1, device_id={"head": head_at(d)}, device_id_type=MESH)
    for d in range(1, chips):
        pl.semaphore_signal(
            barrier, inc=1, device_id={"ctx": chip_at(d) * 2 + core}, device_id_type=MESH
        )
    pl.semaphore_signal(barrier, inc=1, device_id={"ctx": sibling}, device_id_type=MESH)
    pl.semaphore_wait(barrier, nhead - 1 + chips)

    own_cot().wait()
    for d in range(1, nhead):
        cot_copy(d).start()

    @pl.loop(0, heads)
    def _(h):
        own_k(h).wait()
        own_v(h).wait()
        for d in range(1, chips):
            direct(h, d).start()
        forward(h, 0).start()

    @pl.loop(0, heads)
    def _(h):
        for d in range(1, chips):
            arrived(h, core * chips + chip_at(d)).wait_recv()
            forward(h, d).start()
        for c in range(chips):
            arrived(h, other * chips + c).wait_recv()
        qh = q[:, cols(h)]

        def scores(i, best):
            s = mm(kv[h, i, 0], qh, NT)
            s = s.reshape(bpr, BLOCK, rows) + bias[i][:, None, :]
            s = s.reshape(rows, rows)
            sbuf[i] = s
            return jnp.maximum(best, jnp.max(s.reshape(rows // 8, 8, rows), axis=0))

        best = lax.fori_loop(
            0, n, scores, jnp.full((8, rows), 2 * NEG, jnp.float32), unroll=unroll
        )
        best = jnp.max(best, axis=0, keepdims=True)

        def weigh(i, carry):
            total, acc = carry
            p = jnp.exp2((sbuf[i] - best) * SCALE2)
            total = total + jnp.sum(p.reshape(rows // 8, 8, rows), axis=0)
            pb = p.astype(jnp.bfloat16)
            probs[h, i] = pb
            return total, acc + mm(kv[h, i, 1], pb, TN)

        total, acc = lax.fori_loop(
            0, n, weigh,
            (jnp.zeros((8, rows), jnp.float32), jnp.zeros((SIZE, rows), jnp.float32)),
            unroll=unroll,
        )
        scale = 1.0 / jnp.sum(total, axis=0, keepdims=True)
        inv[h] = scale
        out = acc * scale
        att_t[h] = out
        att[:, cols(h)] = out.T.astype(jnp.bfloat16)

    for c in range(nhead):
        load_w(c).wait()
    attended = att[...]
    for d in range(1, nhead):
        mstage[d - 1] = mm(attended, wbuf[head_at(d)], NN).astype(jnp.bfloat16)
        mixed_copy(d).start()

    g_t[...] = mm(wbuf[mh], cbuf[mh], NT)
    for d in range(1, nhead):
        cot_arrived(d).wait_recv()
        g_t[...] += mm(wbuf[head_at(d)], cbuf[head_at(d)], NT)

    def combine(h):
        sib_copy(h).wait_recv()
        for d in range(1, chips + 1):
            c = chip_at(d)
            slot = core * chips + c
            kv[h, slot] = (
                kv[h, slot].astype(jnp.float32) + sib[h, c].astype(jnp.float32)
            ).astype(jnp.bfloat16)
            if d < chips:
                rem_copy(h, d).start()

    @pl.loop(0, heads)
    def _(h):
        for d in range(1, chips):
            direct(h, d).wait_send()
        for d in range(chips):
            forward(h, d).wait_send()
        qh = q[:, cols(h)]
        at = att_t[h].astype(jnp.bfloat16).astype(jnp.float32)
        gt = g_t[pl.ds(pl.multiple_of(h * SIZE, SIZE), SIZE), :].astype(jnp.bfloat16)
        gt = gt.astype(jnp.float32) * inv[h]
        delta = jnp.sum(gt * at, axis=0, keepdims=True)
        gn = gt.T.astype(jnp.bfloat16)
        gt = gt.astype(jnp.bfloat16)

        def step(i, acc):
            kb, vb, pb = kv[h, i, 0], kv[h, i, 1], probs[h, i]
            dp = mm(vb, gt, NN)
            ds = (pb.astype(jnp.float32) * (dp - delta)).astype(jnp.bfloat16)
            kv[h, i, 0] = (mm(ds, qh, NN) * SCALE).astype(jnp.bfloat16)
            kv[h, i, 1] = mm(pb, gn, NN).astype(jnp.bfloat16)
            return acc + mm(kb, ds, TN)

        acc = lax.fori_loop(
            0, n, step, jnp.zeros((SIZE, rows), jnp.float32), unroll=unroll
        )
        qg[:, cols(h)] = (acc.T * SCALE).astype(jnp.bfloat16)
        sib_copy(h).start()

        @pl.when(h > 0)
        def _():
            combine(h - 1)

    combine(heads - 1)

    total = mm(attended, wbuf[mh], NN)
    for d in range(1, nhead):
        mixed_copy(d).wait_recv()
        total += mrecv[d - 1].astype(jnp.float32)
    mixed[...] = total.astype(jnp.bfloat16)

    @pl.loop(0, heads)
    def _(h):
        total = kv[h, mine].astype(jnp.float32)
        for d in range(1, chips):
            rem_copy(h, d).wait_recv()
            total += rem[h, d - 1].astype(jnp.float32)
        kg[:, cols(h)] = total[0].astype(jnp.bfloat16)
        vg[:, cols(h)] = total[1].astype(jnp.bfloat16)

    for d in range(1, nhead):
        cot_copy(d).wait_send()
        mixed_copy(d).wait_send()

    @pl.loop(0, heads)
    def _(h):
        sib_copy(h).wait_send()
        for d in range(1, chips):
            rem_copy(h, d).wait_send()


def hand_over(a, b, c, d, a_out, b_out, c_out, d_out, held, sems):
    def taken(i, src):
        return pltpu.make_async_copy(src, held.at[i], sems.at[0, i])

    def given(i, dst):
        return pltpu.make_async_copy(held.at[i], dst, sems.at[1, i])

    sources, targets = (a, b, c, d), (a_out, b_out, c_out, d_out)
    for i in range(4):
        taken(i, sources[i]).start()
    for i in range(4):
        taken(i, sources[i]).wait()
        given(i, targets[i]).start()
    for i in range(4):
        given(i, targets[i]).wait()


def per_device(queries, keys, values, out_weight, cotangent, contacts, chains):
    rows, width = queries.shape
    heads = width // SIZE
    n = lax.axis_size("ctx")
    nhead = lax.axis_size("head")
    chips = n // 2
    bpr = rows // BLOCK
    out = jax.ShapeDtypeStruct((rows, width), jnp.bfloat16)
    vmem = pl.BlockSpec(memory_space=pltpu.VMEM)
    smem = pl.BlockSpec(memory_space=pltpu.SMEM)
    hbm = pl.BlockSpec(memory_space=pl.ANY)
    bf16, f32 = jnp.bfloat16, jnp.float32
    dma = pltpu.SemaphoreType.DMA
    flops = 2 * rows * n * rows * width * 6 + 4 * rows * width * width * nhead
    results = pl.pallas_call(
        functools.partial(kernel, chips, nhead, heads, 4),
        out_shape=(out, out, out, out),
        in_specs=[smem, smem, vmem, hbm, hbm, hbm, hbm],
        out_specs=(vmem, vmem, vmem, vmem),
        scratch_shapes=[
            pltpu.VMEM((n, bpr, rows), f32),
            pltpu.VMEM((heads, n, 2, rows, SIZE), bf16),
            pltpu.VMEM((heads, n, rows, rows), bf16),
            pltpu.VMEM((n, rows, rows), f32),
            pltpu.VMEM((rows, width), bf16),
            pltpu.VMEM((heads, SIZE, rows), f32),
            pltpu.VMEM((heads, 1, rows), f32),
            pltpu.VMEM((width, rows), f32),
            pltpu.VMEM((heads, chips, 2, rows, SIZE), bf16),
            pltpu.VMEM((heads, chips - 1, 2, rows, SIZE), bf16),
            pltpu.VMEM((nhead, width, width), bf16),
            pltpu.VMEM((nhead, rows, width), bf16),
            pltpu.VMEM((nhead - 1, rows, width), bf16),
            pltpu.VMEM((nhead - 1, rows, width), bf16),
            dma((2, heads)),
            dma((nhead,)),
            dma,
            dma((heads, 2 * chips - 1)),
            dma((heads, n)),
            dma((nhead - 1,)),
            dma((nhead,)),
            dma((nhead - 1,)),
            dma((nhead - 1,)),
            dma((heads,)),
            dma((heads,)),
            dma((heads, chips - 1)),
            dma((heads, chips - 1)),
        ],
        compiler_params=pltpu.CompilerParams(
            collective_id=0, has_side_effects=True, vmem_limit_bytes=60 * 2**20
        ),
        cost_estimate=pl.CostEstimate(
            flops=flops, bytes_accessed=16 * rows * width, transcendentals=rows * n * rows * heads
        ),
        name="attention",
    )(chains, contacts, queries, keys, values, out_weight, cotangent)
    return pl.pallas_call(
        hand_over,
        out_shape=(out, out, out, out),
        in_specs=[hbm] * 4,
        out_specs=(hbm,) * 4,
        scratch_shapes=[pltpu.VMEM((4, rows, width), bf16), dma((2, 4))],
        name="hand_over",
    )(*results)


def solution(mesh):
    split = P("ctx", "head")
    return jax.shard_map(
        per_device,
        mesh=mesh,
        in_specs=(split, split, split, P("head", None), split, P(), P()),
        out_specs=(split, split, split, split),
        check_vma=False,
    )
```
